256 devices in a mesh: grp: 32 (over z, y), tp: 8 (over x, core).
Axes of the slice: x: 4, y: 4, z: 8, core: 2. Of those that a mesh axis runs over, the one named last changes fastest.
Arguments:
- queries: bfloat16 [512, 6144], P('grp', 'tp'), may hold values from -16 to 16
- new_keys: bfloat16 [512, 1024], P('grp', 'tp'), may hold values from -4 to 4
- new_values: bfloat16 [512, 1024], P('grp', 'tp'), may hold values from -4 to 4
- key_cache: bfloat16 [512, 256, 1024], P('grp', None, 'tp'), may hold values from -16 to 16
- value_cache: bfloat16 [512, 256, 1024], P('grp', None, 'tp'), may hold values from -4 to 4
- cache_lengths: int32 [512], P('grp'), may hold values from 2 to 256
- hidden_b: bfloat16 [512, 6144], P('grp', 'tp'), may hold values from -400 to 400
- norm_gain: float32 [6144], replicated, may hold values from 0.5 to 2
- routes: int32 [512, 2], P('grp'), may hold values from 0 to 3, all different within a row; in each aligned block of 16 rows (0 to 15, 16 to 31, ...) at most 12 rows name the same one
- route_gates: float32 [512, 2], P('grp'), may hold values from 0.5 to 1.5
- w_gate: bfloat16 [32, 6144, 2048], P('grp', None, 'tp'), may hold values from -0.078125 to 0.078125
- w_up: bfloat16 [32, 6144, 2048], P('grp', None, 'tp'), may hold values from -0.078125 to 0.078125
- w_down: bfloat16 [32, 2048, 6144], P('grp', 'tp'), may hold values from -0.046875 to 0.046875
Outputs:
- attention_a: bfloat16 [512, 6144], P('grp', 'tp')
- expert_b: bfloat16 [512, 6144], P('grp', 'tp')
The draws below stay inside these ranges and needn't reach their ends.
Inputs may be any that keep to these rules, and one draw needn't show every extreme that they name: `routes`: each row names 2 different experts. In each aligned block of 16 rows (the rows of one index of grp) no expert is named by more than 12 rows.
All inputs are finite; a program needn't handle non-finite values.
Results may differ from the reference program's by a relative error of at most 0.0065.
Values may be sent and summed in bfloat16 or wider, within the bound.
No kernel may reach another device: no remote copies, remote signals or barrier semaphores. Data moves between devices by JAX's collectives and lax.ppermute only.
A program may use at most 128 MiB of HBM per device.

```python
import math
import jax
import jax.numpy as jnp
import numpy as np
from jax import lax

D = 6144
HEADS = 48
KV_HEADS = 8
HEAD_DIM = 128
EXPERTS = 4
FF = 16384
TOP = 2
CTX = 256
MB_DEV = 16
CAP = 12
REQS = 512
FF_SLICE = 2048
N_GRP = 32


def draw_queries(key, part):
    key = jax.random.fold_in(key, 11)
    values = jnp.clip(jax.random.normal(key, (REQS, HEADS * HEAD_DIM), jnp.float32), -4.0, 4.0)
    return values.astype(jnp.bfloat16)


def draw_key_cache(key, part):
    key = jax.random.fold_in(key, 12)
    values = jnp.clip(jax.random.normal(key, (REQS, CTX, KV_HEADS * HEAD_DIM), jnp.float32), -4.0, 4.0)
    return values.astype(jnp.bfloat16)


def draw_cache_lengths(key, part):
    key = jax.random.fold_in(key, 13)
    lengths = jax.random.randint(key, (REQS,), 2, CTX + 1, dtype=jnp.int32)
    return lengths.at[0].set(CTX)


def draw_hidden_b(key, part):
    key = jax.random.fold_in(key, 14)
    key_cols, key_rows, key_base = jax.random.split(key, 3)
    col_scale = jnp.exp(jax.random.uniform(key_cols, (D,), jnp.float32, 0.0, math.log(10.0)))
    row_scale = jnp.exp(jax.random.uniform(key_rows, (REQS,), jnp.float32, 0.0, math.log(10.0)))
    base_draw = jnp.clip(jax.random.normal(key_base, (REQS, D), jnp.float32), -4.0, 4.0)
    return (base_draw * row_scale[:, None] * col_scale[None, :]).astype(jnp.bfloat16)


def block_scale(stream_key, extent, cuts, low, top_value):
    def one(position, parts):
        heights = jax.random.uniform(jax.random.fold_in(jax.random.fold_in(stream_key, 6), position), (parts,), jnp.float32, low / len(cuts), top_value / len(cuts))
        return jnp.repeat(jnp.exp(heights), extent[position] // parts).reshape((-1,) + (1,) * (len(extent) - position - 1))

    level = one(*cuts[0])
    for cut in cuts[1:]:
        level = level * one(*cut)
    return level


def deal_out(rng, own, number, rows, count, top, reach, slope):
    ranking = jax.random.permutation(rng, count)
    packed, ordinary = shares(count, rows * top, reach, slope, True), shares(count, rows * top, reach, slope, False)
    places = jnp.arange(count)

    def named(tallies, rotation):
        used = int((tallies > 0).sum())
        fixed = max(1, used // 4)
        shifted = fixed + (places - fixed + rotation * (used - fixed)) % max(1, count - fixed)
        return jnp.zeros((count,), jnp.int32).at[ranking[jnp.where(places < fixed, places, shifted)]].set(jnp.asarray(tallies, jnp.int32))

    tallies = jnp.where(number % 4 == 0, named(packed, number // 4), named(ordinary, number - number // 4 - 1))
    mixed = jax.random.permutation(jax.random.fold_in(own, 3), count)
    giver, sink = mixed[0:count // 2 * 2:2], mixed[1:count // 2 * 2:2]
    slack = jnp.minimum(tallies[giver] - 1, reach - tallies[sink]) // 2
    slack = jnp.where((giver == ranking[0]) | (sink == ranking[0]) | (tallies[sink] == 0), 0, jnp.maximum(slack, 0))
    shifted = jax.random.randint(jax.random.fold_in(own, 4), (count // 2,), 0, 1 << 20) % (slack + 1)
    tallies = tallies.at[giver].add(-shifted).at[sink].add(shifted)
    items = jnp.searchsorted(jnp.cumsum(tallies), jnp.arange(rows * top), side="right").astype(jnp.int32)
    table = items.reshape(top, rows).T
    table = table[jax.random.permutation(jax.random.fold_in(own, 1), rows)]
    rotation = jax.random.randint(jax.random.fold_in(own, 2), (rows, 1), 0, top)
    return jnp.take_along_axis(table, (jnp.arange(top)[None, :] + rotation) % top, axis=1)


def shares(amount, total, most, lean, full):
    weights = [(1 << 20) // math.isqrt(standing ** lean) + 1 for standing in range(1, amount + 1)]
    largest = most if full else min(most, max(-(-total // amount), total * weights[0] // sum(weights)))
    least = 1 if total - largest >= amount - 1 else 0
    counts, rest = [largest] + [least] * (amount - 1), total - largest - least * (amount - 1)
    while rest > 0:
        free = [i for i in range(1, amount) if counts[i] < largest] or [i for i in range(1, amount) if counts[i] < most]
        pool, budget = sum([weights[i] for i in free]), rest
        for i in free:
            extra = min(most - counts[i], max(1, budget * weights[i] // pool), rest)
            counts[i] = counts[i] + extra
            rest = rest - extra
    return np.array(counts)


def gaussian(stream_key, shape, width, bound, shards=(), held_as=jnp.bfloat16):
    gain = block_scale(stream_key, shape, shards, -0.22, 0.18) if shards else 1.0
    result = jax.random.normal(stream_key, shape, jnp.float32) * width * gain
    return jnp.minimum(jnp.maximum(result, -bound), bound).astype(held_as)


def setup_inputs(seed: int = 0) -> dict:
    splits = jax.random.split(jax.random.key(seed), 14)
    queries = draw_queries(jax.random.fold_in(splits[13], 71), 0)
    new_keys = gaussian(splits[1], (REQS, KV_HEADS * HEAD_DIM), 1.0, 4.0, ((0, 32), (1, 8)))
    new_values = gaussian(splits[2], (REQS, KV_HEADS * HEAD_DIM), 1.0, 4.0, ((0, 32), (1, 8)))
    key_cache = draw_key_cache(jax.random.fold_in(splits[13], 71), 0)
    value_cache = gaussian(splits[4], (REQS, CTX, KV_HEADS * HEAD_DIM), 1.0, 4.0, ((0, 32), (2, 8)))
    cache_lengths = draw_cache_lengths(jax.random.fold_in(splits[13], 71), 0)
    hidden_b = draw_hidden_b(jax.random.fold_in(splits[13], 71), 0)
    norm_gain = jnp.clip(jnp.exp(jax.random.uniform(splits[7], (D,), jnp.float32, math.log(0.5), math.log(2.0))), 0.5, 2.0)
    routes_keys = jax.random.split(jax.random.fold_in(splits[8], 1), REQS // MB_DEV)
    routes_turns = jax.random.permutation(jax.random.fold_in(splits[8], 3), REQS // MB_DEV)
    routes = jax.vmap(lambda own, number: deal_out(jax.random.fold_in(splits[8], 2), own, number, MB_DEV, EXPERTS, TOP, CAP, 1))(routes_keys, routes_turns).reshape((REQS, TOP))
    route_gates = jnp.clip(0.5 + 1.0 * jax.random.uniform(splits[9], (REQS, TOP), jnp.float32) ** block_scale(splits[9], (REQS, TOP), ((0, 32),), -0.2, 0.2), 0.5, 1.5)
    w_gate = gaussian(splits[10], (N_GRP, D, FF_SLICE), D ** -0.5, 0.078125, ((0, 32), (2, 8)))
    w_up = gaussian(splits[11], (N_GRP, D, FF_SLICE), D ** -0.5, 0.078125, ((0, 32), (2, 8)))
    w_down = gaussian(splits[12], (N_GRP, FF_SLICE, D), FF ** -0.5, 0.046875, ((0, 32), (1, 8)))
    return dict(queries=queries, new_keys=new_keys, new_values=new_values, key_cache=key_cache, value_cache=value_cache, cache_lengths=cache_lengths, hidden_b=hidden_b, norm_gain=norm_gain, routes=routes, route_gates=route_gates, w_gate=w_gate, w_up=w_up, w_down=w_down)


def attend(queries, new_keys, new_values, key_cache, value_cache, cache_lengths):
    per_group = HEADS // KV_HEADS
    query_heads = queries.astype(jnp.float32).reshape(REQS, KV_HEADS, per_group, HEAD_DIM)
    key_heads = key_cache.astype(jnp.float32).reshape(REQS, CTX, KV_HEADS, HEAD_DIM)
    value_heads = value_cache.astype(jnp.float32).reshape(REQS, CTX, KV_HEADS, HEAD_DIM)
    own_key = new_keys.astype(jnp.float32).reshape(REQS, KV_HEADS, HEAD_DIM)
    own_value = new_values.astype(jnp.float32).reshape(REQS, KV_HEADS, HEAD_DIM)
    inv_root = 1.0 / HEAD_DIM ** 0.5
    scores = jnp.einsum('rkgd,rckd->rkgc', query_heads, key_heads) * inv_root
    own_score = jnp.einsum('rkgd,rkd->rkg', query_heads, own_key) * inv_root
    visible = (jnp.arange(CTX, dtype=jnp.int32)[None, :] < cache_lengths[:, None])[:, None, None, :]
    scores = jnp.where(visible, scores, -1e+30)
    peak_score = jnp.maximum(lax.optimization_barrier(jnp.max(scores, axis=-1)), own_score)
    weights = jnp.where(visible, jnp.exp(scores - peak_score[..., None]), 0.0)
    own_weight = jnp.exp(own_score - peak_score)
    denominator = lax.optimization_barrier(jnp.sum(weights, axis=-1)) + own_weight
    probabilities = (weights / denominator[..., None]).astype(jnp.bfloat16)
    own_prob = (own_weight / denominator).astype(jnp.bfloat16)
    mixed = jnp.einsum('rkgc,rckd->rkgd', probabilities.astype(jnp.float32), value_heads)
    mixed = mixed + own_prob.astype(jnp.float32)[..., None] * own_value[:, :, None, :]
    return mixed.astype(jnp.bfloat16).reshape(REQS, HEADS * HEAD_DIM)

def experts_layer(hidden_b, norm_gain, routes, route_gates, w_gate, w_up, w_down):
    values = hidden_b.astype(jnp.float32)
    mean_square = lax.optimization_barrier(jnp.mean(values * values, axis=1, keepdims=True))
    normed = (values * lax.rsqrt(mean_square + 1e-05) * norm_gain[None, :]).astype(jnp.bfloat16)
    chosen = routes.reshape(N_GRP, MB_DEV * TOP).astype(jnp.int32)
    onehot = (chosen[:, :, None] == jnp.arange(EXPERTS, dtype=jnp.int32)[None, None, :]).astype(jnp.int32)
    rank_run = jnp.cumsum(onehot, axis=1) - onehot
    slot_ids = lax.optimization_barrier(jnp.sum(rank_run * onehot, axis=2)).astype(jnp.int32)
    owner_row = (jnp.arange(MB_DEV * TOP, dtype=jnp.int32) // TOP).astype(jnp.int32)
    local_rows = normed.reshape(N_GRP, MB_DEV, D)

    def place_rows(rows_here, experts_here, slots_here):
        zero_buffer = jnp.zeros((EXPERTS, CAP, D), jnp.bfloat16)
        return zero_buffer.at[experts_here, slots_here].set(rows_here[owner_row])
    buffers = jax.vmap(place_rows)(local_rows, chosen, slot_ids)
    copies = N_GRP // EXPERTS
    outputs = []
    for expert in range(EXPERTS):
        rows_in = buffers[:, expert].reshape(N_GRP * CAP, D)
        gate_full = jnp.transpose(w_gate[expert::EXPERTS], (1, 0, 2)).reshape(D, copies * FF_SLICE)
        up_full = jnp.transpose(w_up[expert::EXPERTS], (1, 0, 2)).reshape(D, copies * FF_SLICE)
        down_full = w_down[expert::EXPERTS].reshape(copies * FF_SLICE, D)
        gate_sum = jnp.dot(rows_in, gate_full, preferred_element_type=jnp.float32)
        up_sum = jnp.dot(rows_in, up_full, preferred_element_type=jnp.float32)
        activated = (jax.nn.silu(gate_sum) * up_sum).astype(jnp.bfloat16)
        outputs.append(jnp.dot(activated, down_full, preferred_element_type=jnp.float32).reshape(N_GRP, CAP, D))
    stacked = jnp.stack(outputs, axis=1)

    def pick_rows(out_here, experts_here, slots_here):
        return out_here[experts_here, slots_here]
    picked = jax.vmap(pick_rows)(stacked, chosen, slot_ids).reshape(REQS, TOP, D)
    combined = lax.optimization_barrier(jnp.sum(picked * route_gates[:, :, None], axis=1))
    return combined.astype(jnp.bfloat16)

def reference(queries, new_keys, new_values, key_cache, value_cache, cache_lengths, hidden_b, norm_gain, routes, route_gates, w_gate, w_up, w_down):
    attention_a = attend(queries, new_keys, new_values, key_cache, value_cache, cache_lengths)
    expert_b = experts_layer(hidden_b, norm_gain, routes, route_gates, w_gate, w_up, w_down)
    return (attention_a, expert_b)
```

```python
import jax
import jax.numpy as jnp
from jax import lax
from jax.experimental import pallas as pl
from jax.experimental.pallas import tpu as pltpu
from jax.sharding import PartitionSpec as P

HEADS = 48
KV_HEADS = 8
HEAD_DIM = 128
EXPERTS = 4
TOP = 2
NZ, NY, NX = 8, 4, 4
CAP = 12
CHUNKS = ((0, 1, -1, 2), (-2, 3, -3, 4))
VMEM = pl.BlockSpec(memory_space=pltpu.VMEM)
SMEM = pl.BlockSpec(memory_space=pltpu.SMEM)


def attend(queries, new_keys, new_values, key_cache, value_cache, cache_lengths):
    row_count = queries.shape[0]
    slot_count = key_cache.shape[1]
    kv_local = new_keys.shape[1] // HEAD_DIM
    per_group = HEADS // KV_HEADS
    query_heads = queries.reshape(row_count, kv_local, per_group, HEAD_DIM)
    key_heads = key_cache.reshape(row_count, slot_count, kv_local, HEAD_DIM)
    value_heads = value_cache.reshape(row_count, slot_count, kv_local, HEAD_DIM)
    own_key = new_keys.reshape(row_count, kv_local, HEAD_DIM)
    own_value = new_values.reshape(row_count, kv_local, HEAD_DIM)
    inv_root = 1.0 / HEAD_DIM**0.5
    scores = (
        jnp.einsum("rkgd,rckd->rkgc", query_heads, key_heads, preferred_element_type=jnp.float32)
        * inv_root
    )
    own_score = (
        jnp.einsum("rkgd,rkd->rkg", query_heads, own_key, preferred_element_type=jnp.float32)
        * inv_root
    )
    visible = (jnp.arange(slot_count, dtype=jnp.int32)[None, :] < cache_lengths[:, None])[
        :, None, None, :
    ]
    scores = jnp.where(visible, scores, -1e30)
    peak_score = jnp.maximum(jnp.max(scores, axis=-1), own_score)
    weights = jnp.where(visible, jnp.exp(scores - peak_score[..., None]), 0.0)
    own_weight = jnp.exp(own_score - peak_score)
    denominator = jnp.sum(weights, axis=-1) + own_weight
    probabilities = (weights / denominator[..., None]).astype(jnp.bfloat16)
    own_prob = (own_weight / denominator).astype(jnp.bfloat16)
    mixed = jnp.einsum(
        "rkgc,rckd->rkgd", probabilities, value_heads, preferred_element_type=jnp.float32
    )
    mixed = (
        mixed
        + own_prob.astype(jnp.float32)[..., None] * own_value.astype(jnp.float32)[:, :, None, :]
    )
    return mixed.astype(jnp.bfloat16).reshape(row_count, kv_local * per_group * HEAD_DIM)


def move_y(value, shift):
    pairs = [
        (z * NY + y, z * NY + (y + shift) % NY) for z in range(NZ) for y in range(NY)
    ]
    return lax.ppermute(value, "grp", pairs)


def move_z(value, shift):
    pairs = [
        (z * NY + y, (z + shift) % NZ * NY + y) for z in range(NZ) for y in range(NY)
    ]
    return lax.ppermute(value, "grp", pairs)


def move_x(value, shift):
    pairs = []
    for x in range(NX):
        pairs.append((x * 2, (x + shift) % NX * 2))
        pairs.append((x * 2 + 1, (x - shift) % NX * 2 + 1))
    return lax.ppermute(value, "tp", pairs)


def swap_core(value):
    return lax.ppermute(value, "tp", [(t, t ^ 1) for t in range(2 * NX)])


def mlp_kernel(places, *refs):
    xs, (gain, w_gate, w_up, w_down), keeps, sends = refs[:8], refs[8:12], refs[12:16], refs[16:20]
    rows, width = xs[0].shape
    gate = up = squares = None
    for i in range(8):
        k = places[i]
        rows_at = pl.ds(pl.multiple_of(k * width, width), width)
        x = xs[i][...].astype(jnp.float32)
        square = jnp.sum(x * x, axis=1, keepdims=True)
        scaled = (x * gain[pl.ds(k, 1), :]).astype(jnp.bfloat16)
        g = jnp.dot(scaled, w_gate[rows_at, :], preferred_element_type=jnp.float32)
        u = jnp.dot(scaled, w_up[rows_at, :], preferred_element_type=jnp.float32)
        gate, up, squares = (g, u, square) if i == 0 else (gate + g, up + u, squares + square)
    inv_scale = lax.rsqrt(squares * (1.0 / (8 * width)) + 1e-05)
    gate = gate * inv_scale
    up = up * inv_scale
    act = (gate / (1.0 + jnp.exp(-gate)) * up).astype(jnp.bfloat16)
    for j in range(4):
        for base, outs in ((8, sends), (12, keeps)):
            k = places[base + j]
            cols_at = pl.ds(pl.multiple_of(k * width, width), width)
            y = jnp.dot(act, w_down[:, cols_at], preferred_element_type=jnp.float32)
            outs[j][...] = y.astype(outs[j].dtype)


def mlp(places, xs, gain, w_gate, w_up, w_down):
    rows, width = xs[0].shape
    return pl.pallas_call(
        mlp_kernel,
        out_shape=[jax.ShapeDtypeStruct((rows, width), jnp.float32)] * 4
        + [jax.ShapeDtypeStruct((rows, width), jnp.bfloat16)] * 4,
        in_specs=[SMEM] + [VMEM] * 12,
        out_specs=[VMEM] * 8,
        compiler_params=pltpu.CompilerParams(vmem_limit_bytes=40 * 1024 * 1024),
    )(places, *xs, gain, w_gate, w_up, w_down)


def route_tables(routes, route_gates, y):
    row_count = routes.shape[0]
    count = row_count * TOP
    chosen = routes.reshape(count)
    order = jnp.arange(count, dtype=jnp.int32)
    earlier = (chosen[:, None] == chosen[None, :]) & (order[None, :] < order[:, None])
    slots = jnp.sum(earlier.astype(jnp.int32), axis=1)
    target = ((chosen - y) & (EXPERTS - 1)) * CAP + slots
    matches = (
        target.reshape(row_count, TOP)[:, :, None]
        == jnp.arange(EXPERTS * CAP, dtype=jnp.int32)[None, None, :]
    ).astype(jnp.float32)
    placing = jnp.sum(matches, axis=1).T.astype(jnp.bfloat16)
    weights = jnp.sum(matches * route_gates[:, :, None], axis=1)
    return placing, weights


def local(
    queries,
    new_keys,
    new_values,
    key_cache,
    value_cache,
    cache_lengths,
    hidden_b,
    norm_gain,
    routes,
    route_gates,
    w_gate,
    w_up,
    w_down,
):
    bf16, f32 = jnp.bfloat16, jnp.float32
    y = lax.axis_index("grp") % NY
    t = lax.axis_index("tp")
    x, c = t // 2, t % 2
    s = 1 - 2 * c
    width = hidden_b.shape[1]
    placing, weights = route_tables(routes, route_gates, y)
    packed = jnp.dot(placing, hidden_b, preferred_element_type=f32).astype(bf16)

    def block(dx, core):
        return ((x + dx) & (NX - 1)) * 2 + core

    places = jnp.stack(
        [block(0, c), block(0, 1 - c), block(-s, c), block(s, 1 - c)]
        + [block(s, c), block(-s, 1 - c), block(2, c), block(2, 1 - c)]
        + [block(2, 1 - c), block(-s, 1 - c), block(s, 1 - c), block(0, 1 - c)]
        + [block(2, c), block(s, c), block(-s, c), block(0, c)]
    ).astype(jnp.int32)
    gain = norm_gain.reshape(8, width)
    gate_part, up_part, down_part = w_gate[0], w_up[0], w_down[0]

    parts = [packed[r * CAP : (r + 1) * CAP] for r in range(NY)]
    arrived = [parts[0]] + [move_y(parts[r], r) for r in (1, 2, 3)]
    rows_y = jnp.concatenate(arrived, axis=0)
    by_z = {}
    for chunk in CHUNKS:
        for shift in chunk:
            by_z[shift] = rows_y if shift == 0 else move_z(rows_y, shift)

    returned = {}
    for chunk in CHUNKS:
        own = jnp.concatenate([by_z[shift] for shift in chunk], axis=0)
        first = move_x(own, 1)
        other = move_x(own, -1)
        second = move_x(first, 1)
        xs = []
        for piece in (own, first, other, second):
            xs += [piece, swap_core(piece)]
        outs = mlp(places, xs, gain, gate_part, up_part, down_part)
        keeps, sends = outs[:4], outs[4:]
        far, ahead, behind, mine = [
            keep + swap_core(send).astype(f32) for keep, send in zip(keeps, sends)
        ]
        relay = move_x(far.astype(bf16), 1)
        back = move_x(behind.astype(bf16), -1)
        last = move_x((ahead + relay.astype(f32)).astype(bf16), 1)
        total = mine + back.astype(f32) + last.astype(f32)
        height = rows_y.shape[0]
        for i, shift in enumerate(chunk):
            piece = total[i * height : (i + 1) * height]
            returned[shift] = piece if shift == 0 else move_z(piece.astype(bf16), -shift).astype(f32)
    summed = returned[0]
    for shift in returned:
        if shift != 0:
            summed = summed + returned[shift]
    rows_back = summed.astype(bf16)
    pieces = [rows_back[r * CAP : (r + 1) * CAP] for r in range(NY)]
    homes = [summed[:CAP]] + [move_y(pieces[r], -r).astype(f32) for r in (1, 2, 3)]
    expert_b = jnp.dot(
        weights,
        jnp.concatenate(homes, axis=0),
        precision=lax.Precision.HIGHEST,
        preferred_element_type=f32,
    ).astype(bf16)
    attention_a = attend(queries, new_keys, new_values, key_cache, value_cache, cache_lengths)
    return (attention_a, expert_b)


def solution(mesh):
    placed = (
        P("grp", "tp"),
        P("grp", "tp"),
        P("grp", "tp"),
        P("grp", None, "tp"),
        P("grp", None, "tp"),
        P("grp"),
        P("grp", "tp"),
        P(),
        P("grp", None),
        P("grp", None),
        P("grp", None, "tp"),
        P("grp", None, "tp"),
        P("grp", "tp", None),
    )
    return jax.shard_map(
        local,
        mesh=mesh,
        in_specs=placed,
        out_specs=(P("grp", "tp"), P("grp", "tp")),
        check_vma=False,
    )
```

```python
import functools

import jax
import jax.numpy as jnp
from jax import lax
from jax.experimental import pallas as pl
from jax.experimental.pallas import tpu as pltpu
from jax.sharding import PartitionSpec as P

HEAD_DIM = 128
EXPERTS = 4
TOP = 2
NZ, NY, NX = 8, 4, 4
CAP = 12
NEAR = (0, 1, -1, 2, -2)
FAR = (3, 4, -3)
VMEM_LIMIT = 24 * 1024 * 1024
VMEM = pl.BlockSpec(memory_space=pltpu.VMEM)
ANY = pl.BlockSpec(memory_space=pl.ANY)
SMEM = pl.BlockSpec(memory_space=pltpu.SMEM)


def attend_kernel(lengths, queries, new_keys, new_values, key_cache, value_cache, out, q_buf, o_buf):
    f32, bf16 = jnp.float32, jnp.bfloat16
    count, slots, depth = key_cache.shape
    heads = queries.shape[1] // depth
    q_buf[...] = jnp.zeros_like(q_buf)
    for h in range(heads):
        q_buf[:, h, :] = queries[:, h * depth : (h + 1) * depth].astype(f32)
    own_keys = new_keys[...].astype(f32)
    own_values = new_values[...].astype(f32)
    inv_root = 1.0 / depth**0.5
    slot = lax.broadcasted_iota(jnp.int32, (q_buf.shape[1], slots), 1)
    for r in range(count):
        q = q_buf[r]
        scores = inv_root * lax.dot_general(
            q.astype(bf16), key_cache[r], (((1,), (1,)), ((), ())), preferred_element_type=f32
        )
        own = inv_root * jnp.sum(q * own_keys[r : r + 1], axis=1, keepdims=True)
        visible = slot < lengths[r]
        peak = jnp.max(jnp.where(visible, scores, -1e30), axis=1, keepdims=True)
        peak = jnp.maximum(peak, own)
        weights = jnp.where(visible, jnp.exp(scores - peak), 0.0)
        own_weight = jnp.exp(own - peak)
        total = jnp.sum(weights, axis=1, keepdims=True) + own_weight
        probs = (weights / total).astype(bf16)
        own_prob = (own_weight / total).astype(bf16).astype(f32)
        mixed = jnp.dot(probs, value_cache[r], preferred_element_type=f32)
        o_buf[r] = mixed + own_prob * own_values[r : r + 1]
    for h in range(heads):
        out[:, h * depth : (h + 1) * depth] = o_buf[:, h, :].astype(bf16)


def attend(queries, new_keys, new_values, key_cache, value_cache, cache_lengths, after):
    count = queries.shape[0]
    return pl.pallas_call(
        lambda *refs: attend_kernel(*refs[:6], *refs[6 + len(after) :]),
        out_shape=jax.ShapeDtypeStruct(queries.shape, queries.dtype),
        in_specs=[SMEM] + [VMEM] * 5 + [ANY] * len(after),
        out_specs=VMEM,
        scratch_shapes=[pltpu.VMEM((count, 8, HEAD_DIM), jnp.float32)] * 2,
        compiler_params=pltpu.CompilerParams(vmem_limit_bytes=8 * 1024 * 1024),
    )(cache_lengths, queries, new_keys, new_values, key_cache, value_cache, *after)


def move_y(value, shift):
    pairs = [
        (z * NY + y, z * NY + (y + shift) % NY) for z in range(NZ) for y in range(NY)
    ]
    return lax.ppermute(value, "grp", pairs)


def move_z(value, shift):
    pairs = [
        (z * NY + y, (z + shift) % NZ * NY + y) for z in range(NZ) for y in range(NY)
    ]
    return lax.ppermute(value, "grp", pairs)


def move_x(value, shift):
    pairs = []
    for x in range(NX):
        pairs.append((x * 2, (x + shift) % NX * 2))
        pairs.append((x * 2 + 1, (x - shift) % NX * 2 + 1))
    return lax.ppermute(value, "tp", pairs)


def swap_core(value):
    return lax.ppermute(value, "tp", [(t, t ^ 1) for t in range(2 * NX)])


def route_kernel(grp, tp, routes_in, gates_in, hidden_in, weights, *rest):
    packed, (routes, gates, hidden, sems) = rest[:EXPERTS], rest[EXPERTS:]
    copies = [
        pltpu.make_async_copy(source, target, sems.at[i])
        for i, (source, target) in enumerate(
            ((routes_in, routes), (gates_in, gates), (hidden_in, hidden))
        )
    ]
    for copy in copies:
        copy.start()
    for copy in copies:
        copy.wait()
    count = hidden.shape[0]
    shape = (EXPERTS * CAP, count)
    line = lax.broadcasted_iota(jnp.int32, shape, 0)
    relative = sum((line >= CAP * r).astype(jnp.int32) for r in range(1, EXPERTS))
    expert = (relative + grp[0]) & (EXPERTS - 1)
    first = routes[0:1, :] == expert
    second = routes[1:2, :] == expert
    member = (first | second).astype(jnp.float32)
    before = lax.broadcasted_iota(jnp.int32, (count, count), 0) < lax.broadcasted_iota(
        jnp.int32, (count, count), 1
    )
    rank = jnp.dot(
        member.astype(jnp.bfloat16),
        before.astype(jnp.float32).astype(jnp.bfloat16),
        preferred_element_type=jnp.float32,
    )
    slot = (line - relative * CAP).astype(jnp.float32)
    place = jnp.where(rank == slot, member, 0.0)
    weights[...] = place * jnp.where(first, gates[0:1, :], gates[1:2, :])
    rows = jnp.dot(
        place.astype(jnp.bfloat16), hidden[...], preferred_element_type=jnp.float32
    )
    for r in range(EXPERTS):
        packed[r][...] = rows[r * CAP : (r + 1) * CAP].astype(jnp.bfloat16)


def route(grp, tp, routes, route_gates, hidden):
    count, width = hidden.shape
    arrays = [routes.T, route_gates.T, hidden]
    return pl.pallas_call(
        route_kernel,
        out_shape=[jax.ShapeDtypeStruct((EXPERTS * CAP, count), jnp.float32)]
        + [jax.ShapeDtypeStruct((CAP, width), jnp.bfloat16)] * EXPERTS,
        in_specs=[SMEM] * 2 + [ANY] * 3,
        out_specs=[VMEM] * (1 + EXPERTS),
        scratch_shapes=[pltpu.VMEM(array.shape, array.dtype) for array in arrays]
        + [pltpu.SemaphoreType.DMA((3,))],
        compiler_params=pltpu.CompilerParams(vmem_limit_bytes=4 * 1024 * 1024),
    )(grp, tp, *[pltpu.with_memory_space_constraint(array, pltpu.HBM) for array in arrays])


def places_of(tp):
    x, c = tp >> 1, tp & 1
    s = 1 - 2 * c

    def block(dx, core):
        return ((x + dx) & (NX - 1)) * 2 + core

    d = 1 - c
    inward = [block(0, c), block(-s, c), block(s, c), block(2, c)]
    inward += [block(0, d), block(s, d), block(-s, d), block(2, d)]
    outward = [block(2, d), block(-s, d), block(s, d), block(0, d)]
    outward += [block(2, c), block(s, c), block(-s, c), block(0, c)]
    return inward, outward


def mlp_kernel(starts, rows, tp, *refs):
    inward, outward = places_of(tp[0])
    count = len(set(ref for ref, _ in starts))
    x_refs, (gain, w_gate, w_up, w_down) = refs[:count], refs[count : count + 4]
    first, second, *keeps = refs[-6:]
    width = x_refs[0].shape[1]

    def block(i):
        ref, start = starts[i]
        return x_refs[ref][start : start + rows, :].astype(jnp.float32)

    squares = None
    for i in range(8):
        x = block(i)
        x = x * x
        part = x[:, 0:128]
        for j in range(1, width // 128):
            part = part + x[:, j * 128 : (j + 1) * 128]
        squares = part if squares is None else squares + part
    mean = jnp.sum(squares, axis=1, keepdims=True) * (1.0 / (8 * width))
    inv_scale = lax.rsqrt(mean + 1e-05)
    gate = up = None
    for i in range(8):
        k = inward[i]
        at = pl.ds(pl.multiple_of(k * width, width), width)
        x = block(i) * inv_scale
        normed = jnp.concatenate(
            [
                x[:, j * 128 : (j + 1) * 128] * gain[pl.ds(k * (width // 128) + j, 1), :]
                for j in range(width // 128)
            ],
            axis=1,
        ).astype(jnp.bfloat16)
        g = jnp.dot(normed, w_gate[at, :], preferred_element_type=jnp.float32)
        u = jnp.dot(normed, w_up[at, :], preferred_element_type=jnp.float32)
        gate, up = (g, u) if i == 0 else (gate + g, up + u)
    act = (gate / (1.0 + jnp.exp(-gate)) * up).astype(jnp.bfloat16)

    def down(i):
        at = pl.ds(pl.multiple_of(outward[i] * width, width), width)
        return jnp.dot(act, w_down[:, at], preferred_element_type=jnp.float32)

    for out, picks in ((first, (0, 2)), (second, (1, 3))):
        for j, pick in enumerate(picks):
            out[j * rows : (j + 1) * rows, :] = down(pick).astype(jnp.bfloat16)
    for j in range(4):
        keeps[j][...] = down(4 + j)


def mlp(tp, xs, rows, gain, w_gate, w_up, w_down, after):
    arrays, starts = [], []
    for array, start in xs:
        same = [i for i, other in enumerate(arrays) if other is array]
        if not same:
            arrays.append(array)
        starts.append((same[0] if same else len(arrays) - 1, start))
    width = arrays[0].shape[1]
    return pl.pallas_call(
        functools.partial(mlp_kernel, tuple(starts), rows),
        out_shape=[
            jax.ShapeDtypeStruct((2 * rows, width), jnp.bfloat16),
            jax.ShapeDtypeStruct((2 * rows, width), jnp.bfloat16),
        ]
        + [jax.ShapeDtypeStruct((rows, width), jnp.float32)] * 4,
        in_specs=[SMEM] + [VMEM] * (len(arrays) + 4) + [ANY] * len(after),
        out_specs=[VMEM] * 6,
        compiler_params=pltpu.CompilerParams(vmem_limit_bytes=VMEM_LIMIT),
    )(tp, *arrays, gain, w_gate, w_up, w_down, *after)


def join_kernel(groups, *refs):
    out, start = refs[-1], 0
    for rows, terms in groups:
        total = None
        for ref, at in terms:
            value = refs[ref][at : at + rows, :]
            if len(terms) > 1:
                value = value.astype(jnp.float32)
            total = value if total is None else total + value
        out[start : start + rows, :] = total.astype(out.dtype)
        start += rows


def join(groups, after=(), hold=()):
    arrays, plan = [], []
    for rows, terms in groups:
        places = []
        for array, at in terms:
            same = [i for i, other in enumerate(arrays) if other is array]
            if not same:
                arrays.append(array)
            places.append((same[0] if same else len(arrays) - 1, at))
        plan.append((rows, tuple(places)))
    total = sum(rows for rows, _ in plan)
    return pl.pallas_call(
        functools.partial(join_kernel, tuple(plan)),
        out_shape=jax.ShapeDtypeStruct((total, arrays[0].shape[1]), jnp.bfloat16),
        in_specs=[VMEM] * (len(arrays) + len(hold)) + [ANY] * len(after),
        out_specs=VMEM,
        compiler_params=pltpu.CompilerParams(vmem_limit_bytes=8 * 1024 * 1024),
    )(*arrays, *hold, *after)


def local(
    queries,
    new_keys,
    new_values,
    key_cache,
    value_cache,
    cache_lengths,
    hidden_b,
    norm_gain,
    routes,
    route_gates,
    w_gate,
    w_up,
    w_down,
):
    bf16, f32 = jnp.bfloat16, jnp.float32
    width = hidden_b.shape[1]
    tp = lax.axis_index("tp").reshape(1)
    gain = norm_gain.reshape(8 * width // 128, 128)
    gate_part, up_part, down_part = w_gate[0], w_up[0], w_down[0]
    weights, *packed = route(
        lax.axis_index("grp").reshape(1), tp, routes, route_gates, hidden_b
    )

    arrived = [packed[0]] + [move_y(packed[r], r) for r in (1, 2, 3)]
    rows_y = lax.optimization_barrier(jnp.concatenate(arrived, axis=0))
    height = rows_y.shape[0]
    by_z = [(0, rows_y)] + [(shift, move_z(rows_y, shift)) for shift in NEAR[1:]]
    z = dict(by_z)

    def experts(xs, rows, after):
        return mlp(tp, xs, rows, gain, gate_part, up_part, down_part, after)

    a, b = len(NEAR) * height, len(FAR) * height
    own_a = join([(height, [(z[shift], 0)]) for shift in NEAR])
    p1_a = move_x(own_a, 1)
    p3_a = move_x(own_a, -1)
    ahead = move_z(join([(height, [(z[1], 0)]), (height, [(z[2], 0)])]), 2)
    behind = move_z(z[-1], -2)
    own_b = join([(2 * height, [(ahead, 0)]), (height, [(behind, 0)])])
    swap_1 = swap_core(join([(a, [(own_a, 0)]), (a, [(p1_a, 0)]), (a, [(p3_a, 0)])], (), [down_part]))
    both_in = join([(a, [(p1_a, 0)]), (b, [(own_b, 0)])], [p3_a])
    both = move_x(both_in, 1)
    p3_b = move_x(own_b, -1)
    attention_a = attend(
        queries, new_keys, new_values, key_cache, value_cache, cache_lengths, [both_in, own_b]
    )
    done = pltpu.with_memory_space_constraint(attention_a, pltpu.HBM)
    p2_in = join([(b, [(both, a)])], [p3_b])
    p2_b = move_x(p2_in, 1)
    swap_3 = swap_core(p2_b)
    swap_2 = swap_core(
        join([(a + b, [(both, 0)]), (b, [(own_b, 0)]), (b, [(p3_b, 0)])], [done, p2_in])
    )

    xs = [(own_a, 0), (p1_a, 0), (p3_a, 0), (both, 0)]
    xs += [(swap_1, 0), (swap_1, a), (swap_1, 2 * a), (swap_2, 0)]
    send_1, send_2, *keep_a = experts(xs, a, [p2_b])
    got_1, got_2a = swap_core(send_1), swap_core(send_2)
    far_a = join([(a, [(keep_a[0], 0), (got_1, 0)])])
    behind_a = join([(a, [(keep_a[2], 0), (got_1, a)])])
    relay_a = move_x(far_a, 1)
    back_a = move_x(behind_a, -1)

    xs = [(own_b, 0), (both, a), (p3_b, 0), (p2_b, 0)]
    xs += [(swap_2, a + b), (swap_2, a), (swap_2, a + 2 * b), (swap_3, 0)]
    send_1, send_2, *keep_b = experts(xs, b, [far_a, behind_a])
    got_1b, got_2b = swap_core(send_1), swap_core(send_2)
    last_a = [(keep_a[1], 0), (got_2a, 0), (relay_a, 0)]
    far_b = join([(b, [(keep_b[0], 0), (got_1b, 0)])])
    both_in = join([(a, last_a)], [back_a, far_b])
    both = move_x(both_in, 1)
    fore_b = move_x(join([(b, [(keep_b[1], 0), (got_2b, 0)])]), 1)
    back_in = join([(b, [(keep_b[2], 0), (got_1b, b)])])
    back_b = move_x(back_in, -1)
    across_b = move_x(join([(b, [(far_b, 0)])], [back_in]), 2)
    mine_a = keep_a[3] + got_2a[a:].astype(f32)
    mine_b = keep_b[3] + got_2b[b:].astype(f32)
    total_a = mine_a + back_a.astype(f32) + both.astype(f32)
    total_b = mine_b + back_b.astype(f32) + fore_b.astype(f32) + across_b.astype(f32)
    returned = {}
    for total, chunk in zip((total_a, total_b), (NEAR, FAR)):
        for i, shift in enumerate(chunk):
            piece = total[i * height : (i + 1) * height]
            if shift == 1:
                terms = [(mine_a, i * height), (back_a, i * height), (both, i * height)]
                piece = join([(height, terms)])
            returned[shift] = piece if shift == 0 else move_z(piece.astype(bf16), -shift).astype(f32)
    summed = returned[0]
    for shift in returned:
        if shift != 0:
            summed = summed + returned[shift]
    rows_back = summed.astype(bf16)
    pieces = [rows_back[r * CAP : (r + 1) * CAP] for r in range(NY)]
    homes = [summed[:CAP]] + [move_y(pieces[r], -r).astype(f32) for r in (1, 2, 3)]
    expert_b = lax.dot_general(
        weights,
        jnp.concatenate(homes, axis=0),
        (((0,), (0,)), ((), ())),
        precision=lax.Precision.HIGHEST,
        preferred_element_type=f32,
    ).astype(bf16)
    return (attention_a, expert_b)


def solution(mesh):
    placed = (
        P("grp", "tp"),
        P("grp", "tp"),
        P("grp", "tp"),
        P("grp", None, "tp"),
        P("grp", None, "tp"),
        P("grp"),
        P("grp", "tp"),
        P(),
        P("grp", None),
        P("grp", None),
        P("grp", None, "tp"),
        P("grp", None, "tp"),
        P("grp", "tp", None),
    )
    return jax.shard_map(
        local,
        mesh=mesh,
        in_specs=placed,
        out_specs=(P("grp", "tp"), P("grp", "tp")),
        check_vma=False,
    )
```

```python
import functools

import jax
import jax.numpy as jnp
from jax import lax
from jax.experimental import pallas as pl
from jax.experimental.pallas import tpu as pltpu
from jax.sharding import PartitionSpec as P

HEAD_DIM = 128
EXPERTS = 4
TOP = 2
NZ, NY, NX = 8, 4, 4
CAP = 12
NEAR = (0, 1, -1, 2, -2)
FAR = (3, 4, -3)
VMEM_LIMIT = 24 * 1024 * 1024
VMEM = pl.BlockSpec(memory_space=pltpu.VMEM)
ANY = pl.BlockSpec(memory_space=pl.ANY)
SMEM = pl.BlockSpec(memory_space=pltpu.SMEM)


def attend_kernel(lengths, queries, new_keys, new_values, key_cache, value_cache, out, q_buf, o_buf):
    f32, bf16 = jnp.float32, jnp.bfloat16
    count, slots, depth = key_cache.shape
    heads = queries.shape[1] // depth
    q_buf[...] = jnp.zeros_like(q_buf)
    for h in range(heads):
        q_buf[:, h, :] = queries[:, h * depth : (h + 1) * depth].astype(f32)
    own_keys = new_keys[...].astype(f32)
    own_values = new_values[...].astype(f32)
    inv_root = 1.0 / depth**0.5
    slot = lax.broadcasted_iota(jnp.int32, (q_buf.shape[1], slots), 1)
    for r in range(count):
        q = q_buf[r]
        scores = inv_root * lax.dot_general(
            q.astype(bf16), key_cache[r], (((1,), (1,)), ((), ())), preferred_element_type=f32
        )
        own = inv_root * jnp.sum(q * own_keys[r : r + 1], axis=1, keepdims=True)
        visible = slot < lengths[r]
        peak = jnp.max(jnp.where(visible, scores, -1e30), axis=1, keepdims=True)
        peak = jnp.maximum(peak, own)
        weights = jnp.where(visible, jnp.exp(scores - peak), 0.0)
        own_weight = jnp.exp(own - peak)
        total = jnp.sum(weights, axis=1, keepdims=True) + own_weight
        probs = (weights / total).astype(bf16)
        own_prob = (own_weight / total).astype(bf16).astype(f32)
        mixed = jnp.dot(probs, value_cache[r], preferred_element_type=f32)
        o_buf[r] = mixed + own_prob * own_values[r : r + 1]
    for h in range(heads):
        out[:, h * depth : (h + 1) * depth] = o_buf[:, h, :].astype(bf16)


def attend(queries, new_keys, new_values, key_cache, value_cache, cache_lengths, after):
    count = queries.shape[0]
    return pl.pallas_call(
        lambda *refs: attend_kernel(*refs[:6], *refs[6 + len(after) :]),
        out_shape=jax.ShapeDtypeStruct(queries.shape, queries.dtype),
        in_specs=[SMEM] + [VMEM] * 5 + [ANY] * len(after),
        out_specs=VMEM,
        scratch_shapes=[pltpu.VMEM((count, 8, HEAD_DIM), jnp.float32)] * 2,
        compiler_params=pltpu.CompilerParams(vmem_limit_bytes=8 * 1024 * 1024),
    )(cache_lengths, queries, new_keys, new_values, key_cache, value_cache, *after)


def move_y(value, shift):
    pairs = [
        (z * NY + y, z * NY + (y + shift) % NY) for z in range(NZ) for y in range(NY)
    ]
    return lax.ppermute(value, "grp", pairs)


def move_z(value, shift):
    pairs = [
        (z * NY + y, (z + shift) % NZ * NY + y) for z in range(NZ) for y in range(NY)
    ]
    return lax.ppermute(value, "grp", pairs)


def move_x(value, shift):
    pairs = []
    for x in range(NX):
        pairs.append((x * 2, (x + shift) % NX * 2))
        pairs.append((x * 2 + 1, (x - shift) % NX * 2 + 1))
    return lax.ppermute(value, "tp", pairs)


def swap_core(value):
    return lax.ppermute(value, "tp", [(t, t ^ 1) for t in range(2 * NX)])


def route_kernel(grp, tp, routes_in, gates_in, hidden_in, weights, *rest):
    packed, (routes, gates, hidden, sems) = rest[:EXPERTS], rest[EXPERTS:]
    copies = [
        pltpu.make_async_copy(source, target, sems.at[i])
        for i, (source, target) in enumerate(
            ((routes_in, routes), (gates_in, gates), (hidden_in, hidden))
        )
    ]
    for copy in copies:
        copy.start()
    for copy in copies:
        copy.wait()
    count = hidden.shape[0]
    shape = (EXPERTS * CAP, count)
    line = lax.broadcasted_iota(jnp.int32, shape, 0)
    relative = sum((line >= CAP * r).astype(jnp.int32) for r in range(1, EXPERTS))
    expert = (relative + grp[0]) & (EXPERTS - 1)
    first = routes[0:1, :] == expert
    second = routes[1:2, :] == expert
    member = (first | second).astype(jnp.float32)
    before = lax.broadcasted_iota(jnp.int32, (count, count), 0) < lax.broadcasted_iota(
        jnp.int32, (count, count), 1
    )
    rank = jnp.dot(
        member.astype(jnp.bfloat16),
        before.astype(jnp.float32).astype(jnp.bfloat16),
        preferred_element_type=jnp.float32,
    )
    slot = (line - relative * CAP).astype(jnp.float32)
    place = jnp.where(rank == slot, member, 0.0)
    weights[...] = place * jnp.where(first, gates[0:1, :], gates[1:2, :])
    rows = jnp.dot(
        place.astype(jnp.bfloat16), hidden[...], preferred_element_type=jnp.float32
    )
    for r in range(EXPERTS):
        packed[r][...] = rows[r * CAP : (r + 1) * CAP].astype(jnp.bfloat16)


def route(grp, tp, routes, route_gates, hidden):
    count, width = hidden.shape
    arrays = [routes.T, route_gates.T, hidden]
    return pl.pallas_call(
        route_kernel,
        out_shape=[jax.ShapeDtypeStruct((EXPERTS * CAP, count), jnp.float32)]
        + [jax.ShapeDtypeStruct((CAP, width), jnp.bfloat16)] * EXPERTS,
        in_specs=[SMEM] * 2 + [ANY] * 3,
        out_specs=[VMEM] * (1 + EXPERTS),
        scratch_shapes=[pltpu.VMEM(array.shape, array.dtype) for array in arrays]
        + [pltpu.SemaphoreType.DMA((3,))],
        compiler_params=pltpu.CompilerParams(vmem_limit_bytes=4 * 1024 * 1024),
    )(grp, tp, *[pltpu.with_memory_space_constraint(array, pltpu.HBM) for array in arrays])


def places_of(tp):
    x, c = tp >> 1, tp & 1
    s = 1 - 2 * c

    def block(dx, core):
        return ((x + dx) & (NX - 1)) * 2 + core

    d = 1 - c
    inward = [block(0, c), block(-s, c), block(s, c), block(2, c)]
    inward += [block(0, d), block(s, d), block(-s, d), block(2, d)]
    outward = [block(2, d), block(-s, d), block(s, d), block(0, d)]
    outward += [block(2, c), block(s, c), block(-s, c), block(0, c)]
    return inward, outward


def mlp_kernel(starts, rows, tp, *refs):
    inward, outward = places_of(tp[0])
    count = len(set(ref for ref, _ in starts))
    x_refs, (gain, w_gate, w_up, w_down) = refs[:count], refs[count : count + 4]
    first, second, *keeps = refs[-6:]
    width = x_refs[0].shape[1]

    def block(i):
        ref, start = starts[i]
        return x_refs[ref][start : start + rows, :].astype(jnp.float32)

    squares = None
    for i in range(8):
        x = block(i)
        x = x * x
        part = x[:, 0:128]
        for j in range(1, width // 128):
            part = part + x[:, j * 128 : (j + 1) * 128]
        squares = part if squares is None else squares + part
    mean = jnp.sum(squares, axis=1, keepdims=True) * (1.0 / (8 * width))
    inv_scale = lax.rsqrt(mean + 1e-05)
    gate = up = None
    for i in range(8):
        k = inward[i]
        at = pl.ds(pl.multiple_of(k * width, width), width)
        x = block(i) * inv_scale
        normed = jnp.concatenate(
            [
                x[:, j * 128 : (j + 1) * 128] * gain[pl.ds(k * (width // 128) + j, 1), :]
                for j in range(width // 128)
            ],
            axis=1,
        ).astype(jnp.bfloat16)
        g = jnp.dot(normed, w_gate[at, :], preferred_element_type=jnp.float32)
        u = jnp.dot(normed, w_up[at, :], preferred_element_type=jnp.float32)
        gate, up = (g, u) if i == 0 else (gate + g, up + u)
    act = (gate / (1.0 + jnp.exp(-gate)) * up).astype(jnp.bfloat16)

    def down(i):
        at = pl.ds(pl.multiple_of(outward[i] * width, width), width)
        return jnp.dot(act, w_down[:, at], preferred_element_type=jnp.float32)

    for out, picks in ((first, (0, 2)), (second, (1, 3))):
        for j, pick in enumerate(picks):
            out[j * rows : (j + 1) * rows, :] = down(pick).astype(jnp.bfloat16)
    for j in range(4):
        keeps[j][...] = down(4 + j)


def mlp(tp, xs, rows, gain, w_gate, w_up, w_down, after):
    arrays, starts = [], []
    for array, start in xs:
        same = [i for i, other in enumerate(arrays) if other is array]
        if not same:
            arrays.append(array)
        starts.append((same[0] if same else len(arrays) - 1, start))
    width = arrays[0].shape[1]
    return pl.pallas_call(
        functools.partial(mlp_kernel, tuple(starts), rows),
        out_shape=[
            jax.ShapeDtypeStruct((2 * rows, width), jnp.bfloat16),
            jax.ShapeDtypeStruct((2 * rows, width), jnp.bfloat16),
        ]
        + [jax.ShapeDtypeStruct((rows, width), jnp.float32)] * 4,
        in_specs=[SMEM] + [VMEM] * (len(arrays) + 4) + [ANY] * len(after),
        out_specs=[VMEM] * 6,
        compiler_params=pltpu.CompilerParams(vmem_limit_bytes=VMEM_LIMIT),
    )(tp, *arrays, gain, w_gate, w_up, w_down, *after)


def join_kernel(groups, *refs):
    out, start = refs[-1], 0
    for rows, terms in groups:
        total = None
        for ref, at in terms:
            value = refs[ref][at : at + rows, :]
            if len(terms) > 1:
                value = value.astype(jnp.float32)
            total = value if total is None else total + value
        out[start : start + rows, :] = total.astype(out.dtype)
        start += rows


def join(groups, after=(), hold=()):
    arrays, plan = [], []
    for rows, terms in groups:
        places = []
        for array, at in terms:
            same = [i for i, other in enumerate(arrays) if other is array]
            if not same:
                arrays.append(array)
            places.append((same[0] if same else len(arrays) - 1, at))
        plan.append((rows, tuple(places)))
    total = sum(rows for rows, _ in plan)
    return pl.pallas_call(
        functools.partial(join_kernel, tuple(plan)),
        out_shape=jax.ShapeDtypeStruct((total, arrays[0].shape[1]), jnp.bfloat16),
        in_specs=[VMEM] * (len(arrays) + len(hold)) + [ANY] * len(after),
        out_specs=VMEM,
        compiler_params=pltpu.CompilerParams(vmem_limit_bytes=8 * 1024 * 1024),
    )(*arrays, *hold, *after)


def local(
    queries,
    new_keys,
    new_values,
    key_cache,
    value_cache,
    cache_lengths,
    hidden_b,
    norm_gain,
    routes,
    route_gates,
    w_gate,
    w_up,
    w_down,
):
    bf16, f32 = jnp.bfloat16, jnp.float32
    width = hidden_b.shape[1]
    tp = lax.axis_index("tp").reshape(1)
    gain = norm_gain.reshape(8 * width // 128, 128)
    gate_part, up_part, down_part = w_gate[0], w_up[0], w_down[0]
    weights, *packed = route(
        lax.axis_index("grp").reshape(1), tp, routes, route_gates, hidden_b
    )

    arrived = [packed[0]] + [move_y(packed[r], r) for r in (1, 2, 3)]
    rows_y = lax.optimization_barrier(jnp.concatenate(arrived, axis=0))
    height = rows_y.shape[0]
    by_z = [(0, rows_y)] + [(shift, move_z(rows_y, shift)) for shift in NEAR[1:]]
    z = dict(by_z)

    def experts(xs, rows, after):
        return mlp(tp, xs, rows, gain, gate_part, up_part, down_part, after)

    a, b = len(NEAR) * height, len(FAR) * height
    own_a = join([(height, [(z[shift], 0)]) for shift in NEAR])
    p1_a = move_x(own_a, 1)
    p3_a = move_x(own_a, -1)
    ahead = move_z(join([(height, [(z[1], 0)]), (height, [(z[2], 0)])]), 2)
    behind = move_z(z[-1], -2)
    own_b = join([(2 * height, [(ahead, 0)]), (height, [(behind, 0)])])
    swap_1 = swap_core(join([(a, [(own_a, 0)]), (a, [(p1_a, 0)]), (a, [(p3_a, 0)])], (), [down_part]))
    both_in = join([(a, [(p1_a, 0)]), (b, [(own_b, 0)])], [p3_a])
    both = move_x(both_in, 1)
    p3_b = move_x(own_b, -1)
    attention_a = attend(
        queries, new_keys, new_values, key_cache, value_cache, cache_lengths, [both_in, own_b]
    )
    done = pltpu.with_memory_space_constraint(attention_a, pltpu.HBM)
    p2_in = join([(b, [(both, a)])], [p3_b])
    p2_b = move_x(p2_in, 1)
    swap_3 = swap_core(p2_b)
    swap_2 = swap_core(
        join([(a + b, [(both, 0)]), (b, [(own_b, 0)]), (b, [(p3_b, 0)])], [done, p2_in])
    )

    xs = [(own_a, 0), (p1_a, 0), (p3_a, 0), (both, 0)]
    xs += [(swap_1, 0), (swap_1, a), (swap_1, 2 * a), (swap_2, 0)]
    send_1, send_2, *keep_a = experts(xs, a, [p2_b])
    got_1, got_2a = swap_core(send_1), swap_core(send_2)
    far_a = join([(a, [(keep_a[0], 0), (got_1, 0)])])
    relay_a = move_x(far_a, 1)

    xs = [(own_b, 0), (both, a), (p3_b, 0), (p2_b, 0)]
    xs += [(swap_2, a + b), (swap_2, a), (swap_2, a + 2 * b), (swap_3, 0)]
    send_1, send_2, *keep_b = experts(xs, b, [far_a])
    got_1b, got_2b = swap_core(send_1), swap_core(send_2)
    behind_a = join([(a, [(keep_a[2], 0), (got_1, a)])], [got_1b])
    back_a = move_x(behind_a, -1)
    last_a = [(keep_a[1], 0), (got_2a, 0), (relay_a, 0)]
    far_b = join([(b, [(keep_b[0], 0), (got_1b, 0)])])
    both_in = join([(a, last_a)], [far_b])
    both = move_x(both_in, 1)
    fore_b = move_x(join([(b, [(keep_b[1], 0), (got_2b, 0)])]), 1)
    back_in = join([(b, [(keep_b[2], 0), (got_1b, b)])])
    back_b = move_x(back_in, -1)
    across_b = move_x(join([(b, [(far_b, 0)])], [back_in]), 2)
    mine_a = keep_a[3] + got_2a[a:].astype(f32)
    mine_b = keep_b[3] + got_2b[b:].astype(f32)
    total_a = mine_a + back_a.astype(f32) + both.astype(f32)
    total_b = mine_b + back_b.astype(f32) + fore_b.astype(f32) + across_b.astype(f32)
    returned = {}
    for total, chunk in zip((total_a, total_b), (NEAR, FAR)):
        for i, shift in enumerate(chunk):
            piece = total[i * height : (i + 1) * height]
            if shift == 1:
                terms = [(mine_a, i * height), (back_a, i * height), (both, i * height)]
                piece = join([(height, terms)])
            returned[shift] = piece if shift == 0 else move_z(piece.astype(bf16), -shift).astype(f32)
    summed = returned[0]
    for shift in returned:
        if shift != 0:
            summed = summed + returned[shift]
    rows_back = summed.astype(bf16)
    pieces = [rows_back[r * CAP : (r + 1) * CAP] for r in range(NY)]
    homes = [summed[:CAP]] + [move_y(pieces[r], -r).astype(f32) for r in (1, 2, 3)]
    expert_b = lax.dot_general(
        weights,
        jnp.concatenate(homes, axis=0),
        (((0,), (0,)), ((), ())),
        precision=lax.Precision.HIGHEST,
        preferred_element_type=f32,
    ).astype(bf16)
    return (attention_a, expert_b)


def solution(mesh):
    placed = (
        P("grp", "tp"),
        P("grp", "tp"),
        P("grp", "tp"),
        P("grp", None, "tp"),
        P("grp", None, "tp"),
        P("grp"),
        P("grp", "tp"),
        P(),
        P("grp", None),
        P("grp", None),
        P("grp", None, "tp"),
        P("grp", None, "tp"),
        P("grp", "tp", None),
    )
    return jax.shard_map(
        local,
        mesh=mesh,
        in_specs=placed,
        out_specs=(P("grp", "tp"), P("grp", "tp")),
        check_vma=False,
    )
```
